32 devices in a mesh: parts: 2 (over y), nodes: 4 (over z), feat: 2 (over x), sub: 2 (over core).
Axes of the slice: x: 2, y: 2, z: 4, core: 2. Of those that a mesh axis runs over, the one named last changes fastest.
Arguments:
- features: bfloat16 [16384, 512], P(('parts', 'nodes'), 'feat'), parts along dimension 0, may hold values from -6 to 6
- fetch_tiles: int32 [8, 4, 16], P(('parts', 'nodes'), None, 'sub'), parts along dimension 0, may hold values from 0 to 15
- edge_weights: bfloat16 [8, 4, 16, 128, 128], P(('parts', 'nodes'), None, 'sub'), parts along dimension 0, may hold values from 0 to 4, as said below
- target_slots: int32 [8, 4, 16], P(('parts', 'nodes'), None, 'sub'), parts along dimension 0, may hold values from 0 to 23
- hub_tiles: int32 [8, 4, 4], P(('parts', 'nodes'), None, 'sub'), parts along dimension 0, may hold values from 0 to 15
- degree: int32 [16384], P(('parts', 'nodes')), parts along dimension 0, may hold values from 16 to 63
- w_self: bfloat16 [512, 512], replicated, may hold values from -0.25 to 0.25
- w_neigh: bfloat16 [512, 512], replicated, may hold values from -0.25 to 0.25
- bias: float32 [512], P('feat'), may hold values from -3 to 3
Outputs:
- embedded: bfloat16 [16384, 512], P(('parts', 'nodes', 'sub'), 'feat'), parts along dimension 0
The draws below stay inside these ranges and needn't reach their ends.
There are 2 independent parts, one for each index of `parts`. The reference program is written for one: setup_inputs(seed, part) draws one part's arguments, and reference() takes and returns one part's arrays. A program takes and returns all parts, laid end to end along the dimension named above; an argument that names none is the same for every part. Nothing has to cross between parts.
Inputs may be any that keep to these rules, and one draw needn't show every extreme that they name: `edge_weights`: most entries are zero; a node row receives some tens of nonzero weights in all.
All inputs are finite; a program needn't handle non-finite values.
Results may differ from the reference program's by a relative error of at most 0.003.
Values may be sent and summed in bfloat16 or wider, within the bound.
A program may use at most 64 MiB of HBM per device.

```python
import jax
import jax.numpy as jnp
from jax import lax

F = 512
TILE = 128
TILES_DEV = 16
FETCH = 8
HUBP = 2
SLOTS = 16
SLOTS_OUT = 24
ROWS = 8192
N_NODES = 4
N_SUB = 2


def draw_edge_weights(key, part):
    key = jax.random.fold_in(key, 7)
    value_key, keep_key = jax.random.split(key)
    share = min(1.0, 40.0 * SLOTS_OUT / (N_NODES * SLOTS * TILE))
    shape = (N_NODES, N_NODES, SLOTS, TILE, TILE)
    values = jax.random.uniform(value_key, shape, jnp.float32, 0.0, 4.0)
    keep = jax.random.uniform(keep_key, shape, jnp.float32) < share
    return jnp.where(keep, values, 0.0).astype(jnp.bfloat16)


def touch_ends(entries, own_key, low, top_value):
    longest = entries.shape.index(max(entries.shape))
    spots = []
    for shift in (0, 1):
        where = [jax.random.randint(jax.random.fold_in(own_key, axis), (), 0, length) for axis, length in enumerate(entries.shape)]
        where[longest] = (where[longest] + shift) % entries.shape[longest]
        spots.append(tuple(where))
    return entries.at[spots[0]].set(low).at[spots[1]].set(top_value)


def block_levels(stream_key, dims, cuts, low, top_value):
    def one(axis_at, blocks):
        heights = jax.random.uniform(jax.random.fold_in(jax.random.fold_in(stream_key, 6), axis_at), (blocks,), jnp.float32, low / len(cuts), top_value / len(cuts))
        return jnp.repeat(jnp.exp(heights), dims[axis_at] // blocks).reshape((-1,) + (1,) * (len(dims) - axis_at - 1))

    factor_of = one(*cuts[0])
    for cut in cuts[1:]:
        factor_of = factor_of * one(*cut)
    return factor_of


def gaussian(rng, extent, scale, bound, pieces=(), held_as=jnp.bfloat16):
    values = jax.random.normal(rng, extent, jnp.float32) * scale
    if len(pieces) > 0:
        values = block_levels(rng, extent, pieces, -0.22, 0.18) * values
    return jnp.clip(values, min=-bound, max=bound).astype(held_as)


def setup_inputs(seed: int = 0, part: int = 0) -> dict:
    streams_of = jax.random.split(jax.random.key(seed), 10)
    part_keys = jax.random.split(jax.random.fold_in(streams_of[9], part), 10)
    return {
        "features": gaussian(part_keys[0], (ROWS, F), 1.0, 6.0, ((0, 4), (1, 2))),
        "fetch_tiles": touch_ends(jax.random.randint(part_keys[1], (N_NODES, N_NODES, SLOTS), 0, TILES_DEV), jax.random.fold_in(part_keys[1], 1), 0, TILES_DEV - 1).astype(jnp.int32),
        "edge_weights": draw_edge_weights(jax.random.fold_in(jax.random.fold_in(streams_of[9], part), 71), part),
        "target_slots": touch_ends(jax.random.randint(part_keys[3], (N_NODES, N_NODES, SLOTS), 0, SLOTS_OUT), jax.random.fold_in(part_keys[3], 1), 0, SLOTS_OUT - 1).astype(jnp.int32),
        "hub_tiles": touch_ends(jax.random.randint(part_keys[4], (N_NODES, N_NODES, N_SUB * HUBP), 0, TILES_DEV), jax.random.fold_in(part_keys[4], 1), 0, TILES_DEV - 1).astype(jnp.int32),
        "degree": touch_ends(jax.random.randint(part_keys[5], (ROWS,), 16, 64), jax.random.fold_in(part_keys[5], 1), 16, 63).astype(jnp.int32),
        "w_self": gaussian(streams_of[6], (F, F), F ** -0.5, 0.25),
        "w_neigh": gaussian(streams_of[7], (F, F), F ** -0.5, 0.25),
        "bias": gaussian(streams_of[8], (F,), 0.5, 3.0, ((0, 2),), jnp.float32),
    }


def reference(features, fetch_tiles, edge_weights, target_slots, hub_tiles, degree, w_self, w_neigh, bias):
    feat_tiles = features.reshape(N_NODES, TILES_DEV, TILE, F)
    source_ids = jnp.arange(N_NODES, dtype=jnp.int32)[:, None]
    slot_core = (jnp.arange(SLOTS, dtype=jnp.int32) // FETCH)[None, :]

    def helper_step(total, helper):
        tiles = fetch_tiles[:, helper, :]
        gathered = feat_tiles[source_ids, tiles]
        weights = edge_weights[helper]
        contrib = jnp.einsum('spij,spjc->spic', weights.astype(jnp.float32), gathered.astype(jnp.float32))
        goal = target_slots[helper]
        back = jnp.maximum(goal - TILES_DEV, 0)
        owner = back // HUBP
        which = back % HUBP
        remote_tile = hub_tiles[owner, helper, slot_core * HUBP + which]
        dest = jnp.where(goal < TILES_DEV, helper * TILES_DEV + goal, owner * TILES_DEV + remote_tile).astype(jnp.int32)
        total = total.at[dest.reshape(-1)].add(contrib.reshape(N_NODES * SLOTS, TILE * F))
        return total, None

    start = jnp.zeros((N_NODES * TILES_DEV, TILE * F), jnp.float32)
    total, unused = lax.scan(helper_step, start, jnp.arange(N_NODES, dtype=jnp.int32))
    summed = total.reshape(ROWS, F)
    agg = (summed / degree.astype(jnp.float32)[:, None]).astype(jnp.bfloat16)
    pre = jnp.dot(features, w_self, preferred_element_type=jnp.float32)
    pre = pre + jnp.dot(agg, w_neigh, preferred_element_type=jnp.float32) + bias[None, :]
    return jnp.maximum(pre, 0.0).astype(jnp.bfloat16)
```

```python
import functools

import jax
import jax.numpy as jnp
from jax import lax
from jax.experimental import pallas as pl
from jax.experimental.pallas import tpu as pltpu
from jax.sharding import PartitionSpec as P

MESH = pl.DeviceIdType.MESH
CHUNKS = 4


def place(way, k):
    return 0 if k == 0 else 2 * k - 1 + way


def kernel(
    n, nf, fetch, hubs,
    feats, edges, fetch_out, w_self, w_neigh, degree, bias, idx, out,
    xbuf, wts, fetch_in, fetch_s, own_proj, inv, acc, acc2, hub_out, hub_in, sib_out, sib_in,
    local_sem, xs, xr, fs, fr, zs, zr, ss, sr, hs, hr, bs, br, *ys,
):
    me = lax.axis_index("nodes")
    mf = lax.axis_index("feat")
    u = lax.axis_index("sub")
    tiles, tile, cols = feats.shape
    half = tiles // 2
    per = half // CHUNKS
    zero = (2 * n - 1) * fetch
    zero2 = n * hubs
    last_at = n * fetch
    prev2_at = last_at + tiles + n * hubs
    last2_at = prev2_at + n * hubs

    def rows(core, c):
        return pl.ds(core * half + c * per, per)

    def remote(src, dst, send, recv, **where):
        return pltpu.make_async_remote_copy(
            src_ref=src, dst_ref=dst, send_sem=send, recv_sem=recv,
            device_id=where, device_id_type=MESH,
        )

    def x_copy(d, c):
        return remote(
            feats.at[rows(u, c)], xbuf.at[d, pl.ds(c * per, per)],
            xs.at[d - 1, c], xr.at[d - 1, c], feat=lax.rem(mf + d, nf),
        )

    def f_copy(d):
        to = lax.rem(me + d, n)
        return remote(fetch_out.at[to], fetch_in.at[d], fs.at[d - 1], fr.at[d - 1], nodes=to)

    def z_copy(way, k, c):
        return remote(
            ys[place(way, k)].at[rows(u, c)], ys[place(way, k + 1)].at[rows(u, c)],
            zs.at[way, k, c], zr.at[way, k, c], nodes=me + 1 if way == 0 else me - 1,
        )

    def s_copy(p, c, core):
        return remote(
            ys[p].at[rows(core, c)], ys[p].at[rows(core, c)], ss.at[p, c], sr.at[p, c], sub=1 - u
        )

    def h_copy(d):
        return remote(
            hub_out.at[d], hub_in.at[d], hs.at[d - 1], hr.at[d - 1], nodes=lax.rem(me + d, n)
        )

    def b_copy(t):
        return remote(sib_out.at[t], sib_in.at[t], bs.at[t], br.at[t], sub=1 - u)

    def exists(way, k):
        return me >= k if way == 0 else me + k < n

    own_copy = pltpu.make_async_copy(feats.at[pl.ds(u * half, half)], xbuf.at[0], local_sem.at[0])
    own_copy.start()
    wts_copy = pltpu.make_async_copy(edges, wts, local_sem.at[1])
    wts_copy.start()

    barrier = pltpu.get_barrier_semaphore()
    for d in range(1, nf):
        pl.semaphore_signal(barrier, inc=1, device_id={"feat": lax.rem(mf + d, nf)}, device_id_type=MESH)
    for d in range(1, n):
        pl.semaphore_signal(barrier, inc=1, device_id={"nodes": lax.rem(me + d, n)}, device_id_type=MESH)
    pl.semaphore_signal(barrier, inc=1, device_id={"sub": 1 - u}, device_id_type=MESH)
    pl.semaphore_wait(barrier, nf + n - 1)

    for c in range(CHUNKS):
        for d in range(1, nf):
            x_copy(d, c).start()
    for d in range(1, n):
        f_copy(d).start()
    fetch_in[0] = fetch_out[me]
    acc[zero] = jnp.zeros((tile, cols), jnp.float32)
    acc2[zero2] = jnp.zeros((tile, cols), jnp.float32)

    def project(w, c):
        total = None
        for d in range(nf):
            start = pl.multiple_of(lax.rem(mf + nf - d, nf) * cols, cols)
            piece = xbuf[d, c * per:(c + 1) * per].reshape(per * tile, cols)
            term = jnp.dot(piece, w[pl.ds(start, cols), :], preferred_element_type=jnp.float32)
            total = term if total is None else total + term
        return total

    own_copy.wait()
    for c in range(CHUNKS):
        for d in range(1, nf):
            x_copy(d, c).wait_recv()
        y = project(w_neigh, c)
        ys[0][rows(u, c)] = y.astype(jnp.bfloat16).reshape(per, tile, cols)
        for way in range(2):
            pl.when(exists(1 - way, 1))(lambda: z_copy(way, 0, c).start())
        s_copy(0, c, u).start()

    for d in range(1, n):
        f_copy(d).wait_recv()
    to_smem = pltpu.make_async_copy(fetch_in, fetch_s, local_sem.at[2])
    to_smem.start()
    diagonal = lax.broadcasted_iota(jnp.int32, (tile, tile), 0) == lax.broadcasted_iota(
        jnp.int32, (tile, tile), 1
    )
    for c in range(CHUNKS):
        own_proj[c * per:(c + 1) * per] = (project(w_self, c) + bias[...]).reshape(per, tile, cols)
    for t in range(half):
        row = 1.0 / degree[pl.ds(u * half + t, 1), :].astype(jnp.float32)
        inv[t] = jnp.sum(
            jnp.where(diagonal, jnp.broadcast_to(row, (tile, tile)), 0.0), axis=1, keepdims=True
        )
    wts_copy.wait()
    to_smem.wait()

    def contribute(way, k):
        p = place(way, k)
        shard = me - k if way == 0 else me + k
        d = k if way == 0 else (n - k) % n
        for c in range(CHUNKS):
            s_copy(p, c, 1 - u).wait_recv()
        for j in range(fetch):
            term = jnp.dot(
                wts[shard, j], ys[p][fetch_s[d, 0, j]], preferred_element_type=jnp.float32
            )
            acc[p * fetch + j] = acc[idx[shard * fetch + j]] + term

    def arrive(way, k, c):
        z_copy(way, k - 1, c).wait_recv()
        if k < n - 1:
            pl.when(exists(1 - way, 1))(lambda: z_copy(way, k, c).start())
        s_copy(place(way, k), c, u).start()

    for k in range(1, n):
        for c in range(CHUNKS):
            for way in range(2):
                pl.when(exists(way, k))(functools.partial(arrive, way, k, c))
            if c == 0:
                if k == 1:
                    contribute(0, 0)
                else:
                    for way in range(2):
                        pl.when(exists(way, k - 1))(functools.partial(contribute, way, k - 1))
    for way in range(2):
        pl.when(exists(way, n - 1))(functools.partial(contribute, way, n - 1))

    for d in list(range(1, n)) + [0]:
        to = lax.rem(me + d, n)
        for k in range(hubs):
            part = acc[idx[last_at + tiles + to * hubs + k]].astype(jnp.bfloat16)
            if d:
                hub_out[d, k] = part
            else:
                hub_in[0, k] = part
        if d:
            h_copy(d).start()

    for d in range(n):
        if d:
            h_copy(d).wait_recv()
        helper = lax.rem(me + n - d, n)
        for k in range(hubs):
            acc2[d * hubs + k] = acc2[idx[prev2_at + helper * hubs + k]] + hub_in[d, k].astype(
                jnp.float32
            )

    def total(t):
        return acc[idx[last_at + t]] + acc2[idx[last2_at + t]]

    for t in range(half):
        sib_out[t] = total((1 - u) * half + t).astype(jnp.bfloat16)
        b_copy(t).start()
    for t in range(half):
        mine = total(u * half + t)
        b_copy(t).wait_recv()
        pre = own_proj[t] + (mine + sib_in[t].astype(jnp.float32)) * inv[t]
        out[t] = jnp.maximum(pre, 0.0).astype(jnp.bfloat16)

    for c in range(CHUNKS):
        for d in range(1, nf):
            x_copy(d, c).wait_send()
    for d in range(1, n):
        f_copy(d).wait_send()
        h_copy(d).wait_send()
    for t in range(half):
        b_copy(t).wait_send()

    def sent(way, k, c):
        s_copy(place(way, k), c, u).wait_send()
        if k < n - 1:
            pl.when(exists(1 - way, 1))(lambda: z_copy(way, k, c).wait_send())

    for c in range(CHUNKS):
        s_copy(0, c, u).wait_send()
        for way in range(2):
            pl.when(exists(1 - way, 1))(lambda: z_copy(way, 0, c).wait_send())
            for k in range(1, n):
                pl.when(exists(way, k))(functools.partial(sent, way, k, c))


def chain(target, key, count, empty):
    same = target[:, None] == target[None, :]
    before = key[None, :] < key[:, None]
    prev = jnp.max(jnp.where(same & before, key[None, :], -1), axis=1)
    hit = target[None, :] == jnp.arange(count, dtype=jnp.int32)[:, None]
    last = jnp.max(jnp.where(hit, key[None, :], -1), axis=1)
    return jnp.where(prev < 0, empty, prev), jnp.where(last < 0, empty, last)


def body(
    features, fetch_tiles, edge_weights, target_slots, hub_tiles, degree, w_self, w_neigh, bias
):
    n = lax.axis_size("nodes")
    nf = lax.axis_size("feat")
    me = lax.axis_index("nodes")
    cols = features.shape[1]
    tile = edge_weights.shape[-1]
    tiles = features.shape[0] // tile
    half = tiles // 2
    fetch = fetch_tiles.shape[2]
    hubs = hub_tiles.shape[2]
    first_col = lax.axis_index("feat") * cols
    self_cols = lax.dynamic_slice_in_dim(w_self, first_col, cols, 1)
    neigh_cols = lax.dynamic_slice_in_dim(w_neigh, first_col, cols, 1)

    shard = jnp.arange(n, dtype=jnp.int32)
    away = jnp.abs(shard - me)
    slot = jnp.where(shard < me, 2 * away - 1, 2 * away)
    key = (slot[:, None] * fetch + jnp.arange(fetch, dtype=jnp.int32)[None, :]).reshape(-1)
    prev, last = chain(target_slots.reshape(-1), key, tiles + n * hubs, (2 * n - 1) * fetch)
    key2 = (
        ((me - shard) % n)[:, None] * hubs + jnp.arange(hubs, dtype=jnp.int32)[None, :]
    ).reshape(-1)
    prev2, last2 = chain(hub_tiles.reshape(-1), key2, tiles, n * hubs)
    idx = jnp.concatenate([prev, last, prev2, last2])
    fetch_out = jnp.zeros((n, 8, 128), jnp.int32).at[:, 0, :fetch].set(fetch_tiles[0])

    bf16, f32 = jnp.bfloat16, jnp.float32
    vmem = pl.BlockSpec(memory_space=pltpu.VMEM)
    hbm = pl.BlockSpec(memory_space=pl.ANY)
    dma = pltpu.SemaphoreType.DMA
    result = pl.pallas_call(
        functools.partial(kernel, n, nf, fetch, hubs),
        out_shape=jax.ShapeDtypeStruct((half, tile, cols), bf16),
        in_specs=[hbm, hbm, vmem, vmem, vmem, vmem, vmem, pl.BlockSpec(memory_space=pltpu.SMEM)],
        out_specs=vmem,
        scratch_shapes=[
            pltpu.VMEM((nf, half, tile, cols), bf16),
            pltpu.VMEM((n, fetch, tile, tile), bf16),
            pltpu.VMEM((n, 8, 128), jnp.int32),
            pltpu.SMEM((n, 8, 128), jnp.int32),
            pltpu.VMEM((half, tile, cols), f32),
            pltpu.VMEM((half, tile, 1), f32),
            pltpu.VMEM(((2 * n - 1) * fetch + 1, tile, cols), f32),
            pltpu.VMEM((n * hubs + 1, tile, cols), f32),
            pltpu.VMEM((n, hubs, tile, cols), bf16),
            pltpu.VMEM((n, hubs, tile, cols), bf16),
            pltpu.VMEM((half, tile, cols), bf16),
            pltpu.VMEM((half, tile, cols), bf16),
            dma((3,)),
            dma((nf - 1, CHUNKS)),
            dma((nf - 1, CHUNKS)),
            dma((n - 1,)),
            dma((n - 1,)),
            dma((2, n - 1, CHUNKS)),
            dma((2, n - 1, CHUNKS)),
            dma((2 * n - 1, CHUNKS)),
            dma((2 * n - 1, CHUNKS)),
            dma((n - 1,)),
            dma((n - 1,)),
            dma((half,)),
            dma((half,)),
        ]
        + [pltpu.VMEM((tiles, tile, cols), bf16) for _ in range(2 * n - 1)],
        compiler_params=pltpu.CompilerParams(
            collective_id=0, has_side_effects=True, vmem_limit_bytes=56 * 1024 * 1024
        ),
        name="sage_layer",
    )(
        features.reshape(tiles, tile, cols), edge_weights[0], fetch_out, self_cols, neigh_cols,
        degree.reshape(tiles, tile), bias.reshape(1, cols), idx,
    )
    return result.reshape(half * tile, cols)


def solution(mesh):
    return jax.shard_map(
        body,
        mesh=mesh,
        in_specs=(
            P(("parts", "nodes"), "feat"),
            P(("parts", "nodes"), None, "sub"),
            P(("parts", "nodes"), None, "sub", None, None),
            P(("parts", "nodes"), None, "sub"),
            P(("parts", "nodes"), None, "sub"),
            P(("parts", "nodes")),
            P(),
            P(),
            P("feat"),
        ),
        out_specs=P(("parts", "nodes", "sub"), "feat"),
        check_vma=False,
    )
```

```python
import functools

import jax
import jax.numpy as jnp
from jax import lax
from jax.experimental import pallas as pl
from jax.experimental.pallas import tpu as pltpu
from jax.sharding import PartitionSpec as P

MESH = pl.DeviceIdType.MESH
CHUNKS = 8


def place(way, k):
    return 0 if k == 0 else 2 * k - 1 + way


def kernel(
    n, nf, fetch, hubs,
    feats, edges, fetch_tiles, targets, hub_tiles, w_self_in, w_neigh_in, degree, bias, out,
    xbuf, wts, w_self, w_neigh, fetch_out, fetch_in, fetch_s, prev, last, prev2, last2, own_proj, inv, acc, acc2, hub_out, hub_in, sib_out, sib_in,
    local_sem, xs, xr, fs, fr, zs, zr, ss, sr, hs, hr, bs, br, *ys,
):
    me = lax.axis_index("nodes")
    mf = lax.axis_index("feat")
    u = lax.axis_index("sub")
    tiles, tile, cols = feats.shape
    half = tiles // 2
    per = half // CHUNKS
    zero = (2 * n - 1) * fetch
    zero2 = n * hubs

    def rows(core, c):
        return pl.ds(core * half + c * per, per)

    def remote(src, dst, send, recv, **where):
        return pltpu.make_async_remote_copy(
            src_ref=src, dst_ref=dst, send_sem=send, recv_sem=recv,
            device_id=where, device_id_type=MESH,
        )

    def x_copy(d, c):
        return remote(
            feats.at[rows(u, c)], xbuf.at[d, pl.ds(c * per, per)],
            xs.at[d - 1, c], xr.at[d - 1, c], feat=lax.rem(mf + d, nf),
        )

    def f_copy(d):
        to = lax.rem(me + d, n)
        return remote(fetch_out.at[to], fetch_in.at[d], fs.at[d - 1], fr.at[d - 1], nodes=to)

    def z_copy(way, k, c):
        return remote(
            ys[place(way, k)].at[rows(u, c)], ys[place(way, k + 1)].at[rows(u, c)],
            zs.at[way, k, c], zr.at[way, k, c], nodes=me + 1 if way == 0 else me - 1,
        )

    def s_copy(p, c, core):
        return remote(
            ys[p].at[rows(core, c)], ys[p].at[rows(core, c)], ss.at[p, c], sr.at[p, c], sub=1 - u
        )

    def h_copy(d):
        return remote(
            hub_out.at[d], hub_in.at[d], hs.at[d - 1], hr.at[d - 1], nodes=lax.rem(me + d, n)
        )

    def b_copy(t):
        return remote(sib_out.at[t], sib_in.at[t], bs.at[t], br.at[t], sub=1 - u)

    def exists(way, k):
        return me >= k if way == 0 else me + k < n

    own_copy = pltpu.make_async_copy(feats.at[pl.ds(u * half, half)], xbuf.at[0], local_sem.at[0])
    own_copy.start()
    w_copies = []
    for i, (whole, part) in enumerate(((w_neigh_in, w_neigh), (w_self_in, w_self))):
        if whole.shape[1] != cols:
            whole = whole.at[:, pl.ds(pl.multiple_of(mf * cols, cols), cols)]
        w_copies.append(pltpu.make_async_copy(whole, part, local_sem.at[3 + i]))
        w_copies[-1].start()
    wts_copy = pltpu.make_async_copy(edges, wts, local_sem.at[1])
    wts_copy.start()

    fetch_out[...] = jnp.zeros_like(fetch_out)
    for t in range(n):
        fetch_out[t, 0:1, 0:fetch] = fetch_tiles[t:t + 1, :]

    barrier = pltpu.get_barrier_semaphore()
    for d in range(1, nf):
        pl.semaphore_signal(barrier, inc=1, device_id={"feat": lax.rem(mf + d, nf)}, device_id_type=MESH)
    for d in range(1, n):
        pl.semaphore_signal(barrier, inc=1, device_id={"nodes": lax.rem(me + d, n)}, device_id_type=MESH)
    pl.semaphore_signal(barrier, inc=1, device_id={"sub": 1 - u}, device_id_type=MESH)
    pl.semaphore_wait(barrier, nf + n - 1)

    for c in range(CHUNKS):
        for d in range(1, nf):
            x_copy(d, c).start()
    for d in range(1, n):
        f_copy(d).start()
    fetch_in[0] = fetch_out[me]
    acc[zero] = jnp.zeros((tile, cols), jnp.float32)
    acc2[zero2] = jnp.zeros((tile, cols), jnp.float32)

    spots = [(0, 0)] + [(way, k) for k in range(1, n) for way in range(2)]

    def link(way, k):
        p = place(way, k)
        shard = me - k if way == 0 else me + k

        def edge(j, carry):
            target = targets[shard, j]
            slot = p * fetch + j
            prev[slot] = last[target]
            for g in range(tiles + n * hubs):
                last[g] = jnp.where(target == g, slot, last[g])
            return carry

        lax.fori_loop(0, fetch, edge, 0)

    def link_hubs():
        for g in range(tiles + n * hubs):
            last[g] = jnp.int32(zero)
        for g in range(tiles):
            last2[g] = jnp.int32(zero2)

        def helper(d, carry):
            row = lax.rem(me + n - d, n)
            for k in range(hubs):
                target = hub_tiles[row, k]
                slot = d * hubs + k
                prev2[slot] = last2[target]
                for g in range(tiles):
                    last2[g] = jnp.where(target == g, slot, last2[g])
            return carry

        lax.fori_loop(0, n, helper, 0)

    def project(w, c):
        total = None
        for d in range(nf):
            start = pl.multiple_of(lax.rem(mf + nf - d, nf) * cols, cols)
            piece = xbuf[d, c * per:(c + 1) * per].reshape(per * tile, cols)
            term = jnp.dot(piece, w[pl.ds(start, cols), :], preferred_element_type=jnp.float32)
            total = term if total is None else total + term
        return total

    own_copy.wait()
    w_copies[0].wait()
    for c in range(CHUNKS):
        for d in range(1, nf):
            x_copy(d, c).wait_recv()
        y = project(w_neigh, c)
        ys[0][rows(u, c)] = y.astype(jnp.bfloat16).reshape(per, tile, cols)
        for way in range(2):
            pl.when(exists(1 - way, 1))(lambda: z_copy(way, 0, c).start())
        s_copy(0, c, u).start()
        if c == 0:
            link_hubs()
        elif c <= len(spots):
            way, k = spots[c - 1]
            pl.when(exists(way, k))(functools.partial(link, way, k))
    for way, k in spots[CHUNKS - 1:]:
        pl.when(exists(way, k))(functools.partial(link, way, k))

    for d in range(1, n):
        f_copy(d).wait_recv()
    to_smem = pltpu.make_async_copy(fetch_in, fetch_s, local_sem.at[2])
    to_smem.start()
    diagonal = lax.broadcasted_iota(jnp.int32, (tile, tile), 0) == lax.broadcasted_iota(
        jnp.int32, (tile, tile), 1
    )
    w_copies[1].wait()
    for c in range(CHUNKS):
        own_proj[c * per:(c + 1) * per] = (project(w_self, c) + bias[...]).reshape(per, tile, cols)
    for t in range(half):
        row = 1.0 / degree[pl.ds(u * half + t, 1), :].astype(jnp.float32)
        inv[t] = jnp.sum(
            jnp.where(diagonal, jnp.broadcast_to(row, (tile, tile)), 0.0), axis=1, keepdims=True
        )
    wts_copy.wait()
    to_smem.wait()

    def contribute(way, k):
        p = place(way, k)
        shard = me - k if way == 0 else me + k
        d = k if way == 0 else (n - k) % n
        for c in range(CHUNKS):
            s_copy(p, c, 1 - u).wait_recv()
        for j in range(fetch):
            term = jnp.dot(
                wts[shard, j], ys[p][fetch_s[d, 0, j]], preferred_element_type=jnp.float32
            )
            acc[p * fetch + j] = acc[prev[p * fetch + j]] + term

    def arrive(way, k, c):
        z_copy(way, k - 1, c).wait_recv()
        if k < n - 1:
            pl.when(exists(1 - way, 1))(lambda: z_copy(way, k, c).start())
        s_copy(place(way, k), c, u).start()

    for k in range(1, n):
        for c in range(CHUNKS):
            for way in range(2):
                pl.when(exists(way, k))(functools.partial(arrive, way, k, c))
            if c == 0:
                if k == 1:
                    contribute(0, 0)
                else:
                    for way in range(2):
                        pl.when(exists(way, k - 1))(functools.partial(contribute, way, k - 1))
    for way in range(2):
        pl.when(exists(way, n - 1))(functools.partial(contribute, way, n - 1))

    def put_hubs(d):
        to = lax.rem(me + d, n)
        for k in range(hubs):
            part = acc[last[tiles + to * hubs + k]].astype(jnp.bfloat16)
            if d:
                hub_out[d, k] = part
            else:
                hub_in[0, k] = part

    def sent(way, k, c):
        z_copy(way, k, c).wait_send()

    for d in range(n):
        put_hubs(d)
    inside = (me > 0) & (me < n - 1)
    for d in range(1, n):
        to = lax.rem(me + d, n)
        pl.when(inside & (to > 0) & (to < n - 1))(lambda: h_copy(d).start())
    for c in range(CHUNKS):
        for way in range(2):
            for k in range(n - 1):
                pl.when(exists(way, k) & exists(1 - way, 1))(functools.partial(sent, way, k, c))
    for d in range(1, n):
        to = lax.rem(me + d, n)
        pl.when(inside & ((to == 0) | (to == n - 1)))(lambda: h_copy(d).start())
        pl.when(me == n - 1)(lambda: h_copy(d).start())
        pl.when(me == 0)(lambda: h_copy(n - d).start())

    for d in range(n):
        if d:
            h_copy(d).wait_recv()
        for k in range(hubs):
            acc2[d * hubs + k] = acc2[prev2[d * hubs + k]] + hub_in[d, k].astype(
                jnp.float32
            )

    def total(t):
        return acc[last[t]] + acc2[last2[t]]

    for t in range(half):
        sib_out[t] = total((1 - u) * half + t).astype(jnp.bfloat16)
        b_copy(t).start()
    for t in range(half):
        mine = total(u * half + t)
        b_copy(t).wait_recv()
        pre = own_proj[t] + (mine + sib_in[t].astype(jnp.float32)) * inv[t]
        out[t] = pre.astype(jnp.bfloat16)

    for c in range(CHUNKS):
        for d in range(1, nf):
            x_copy(d, c).wait_send()
    for d in range(1, n):
        f_copy(d).wait_send()
        h_copy(d).wait_send()
    for t in range(half):
        b_copy(t).wait_send()

    for c in range(CHUNKS):
        s_copy(0, c, u).wait_send()
        for way in range(2):
            for k in range(1, n):
                pl.when(exists(way, k))(lambda: s_copy(place(way, k), c, u).wait_send())


def body(
    features, fetch_tiles, edge_weights, target_slots, hub_tiles, degree, w_self, w_neigh, bias
):
    n = lax.axis_size("nodes")
    nf = lax.axis_size("feat")
    cols = features.shape[1]
    tile = edge_weights.shape[-1]
    tiles = features.shape[0] // tile
    half = tiles // 2
    fetch = fetch_tiles.shape[2]
    hubs = hub_tiles.shape[2]
    if cols % 128:
        first_col = lax.axis_index("feat") * cols
        w_self = lax.dynamic_slice_in_dim(w_self, first_col, cols, 1)
        w_neigh = lax.dynamic_slice_in_dim(w_neigh, first_col, cols, 1)
    depth = w_self.shape[0]

    bf16, f32 = jnp.bfloat16, jnp.float32
    vmem = pl.BlockSpec(memory_space=pltpu.VMEM)
    hbm = pl.BlockSpec(memory_space=pl.ANY)
    smem = pl.BlockSpec(memory_space=pltpu.SMEM)
    dma = pltpu.SemaphoreType.DMA
    result = pl.pallas_call(
        functools.partial(kernel, n, nf, fetch, hubs),
        out_shape=jax.ShapeDtypeStruct((half, tile, cols), bf16),
        in_specs=[hbm, hbm, vmem, smem, smem, hbm, hbm, vmem, vmem],
        out_specs=vmem,
        scratch_shapes=[
            pltpu.VMEM((nf, half, tile, cols), bf16),
            pltpu.VMEM((n, fetch, tile, tile), bf16),
            pltpu.VMEM((depth, cols), bf16),
            pltpu.VMEM((depth, cols), bf16),
            pltpu.VMEM((n, 8, 128), jnp.int32),
            pltpu.VMEM((n, 8, 128), jnp.int32),
            pltpu.SMEM((n, 8, 128), jnp.int32),
            pltpu.SMEM(((2 * n - 1) * fetch,), jnp.int32),
            pltpu.SMEM((tiles + n * hubs,), jnp.int32),
            pltpu.SMEM((n * hubs,), jnp.int32),
            pltpu.SMEM((tiles,), jnp.int32),
            pltpu.VMEM((half, tile, cols), f32),
            pltpu.VMEM((half, tile, 1), f32),
            pltpu.VMEM(((2 * n - 1) * fetch + 1, tile, cols), f32),
            pltpu.VMEM((n * hubs + 1, tile, cols), f32),
            pltpu.VMEM((n, hubs, tile, cols), bf16),
            pltpu.VMEM((n, hubs, tile, cols), bf16),
            pltpu.VMEM((half, tile, cols), bf16),
            pltpu.VMEM((half, tile, cols), bf16),
            dma((5,)),
            dma((nf - 1, CHUNKS)),
            dma((nf - 1, CHUNKS)),
            dma((n - 1,)),
            dma((n - 1,)),
            dma((2, n - 1, CHUNKS)),
            dma((2, n - 1, CHUNKS)),
            dma((2 * n - 1, CHUNKS)),
            dma((2 * n - 1, CHUNKS)),
            dma((n - 1,)),
            dma((n - 1,)),
            dma((half,)),
            dma((half,)),
        ]
        + [pltpu.VMEM((tiles, tile, cols), bf16) for _ in range(2 * n - 1)],
        compiler_params=pltpu.CompilerParams(
            collective_id=0, has_side_effects=True, vmem_limit_bytes=56 * 1024 * 1024
        ),
        name="sage_layer",
    )(
        features.reshape(tiles, tile, cols), edge_weights[0], fetch_tiles[0], target_slots[0],
        hub_tiles[0], w_self, w_neigh, degree.reshape(tiles, tile), bias.reshape(1, cols),
    )
    return jnp.maximum(result.reshape(half * tile, cols), 0)


def solution(mesh):
    return jax.shard_map(
        body,
        mesh=mesh,
        in_specs=(
            P(("parts", "nodes"), "feat"),
            P(("parts", "nodes"), None, "sub"),
            P(("parts", "nodes"), None, "sub", None, None),
            P(("parts", "nodes"), None, "sub"),
            P(("parts", "nodes"), None, "sub"),
            P(("parts", "nodes")),
            P(),
            P(),
            P("feat"),
        ),
        out_specs=P(("parts", "nodes", "sub"), "feat"),
        check_vma=False,
    )
```

```python
import functools

import jax
import jax.numpy as jnp
from jax import lax
from jax.experimental import pallas as pl
from jax.experimental.pallas import tpu as pltpu
from jax.sharding import PartitionSpec as P

MESH = pl.DeviceIdType.MESH
CHUNKS = 8


def place(way, k):
    return 0 if k == 0 else 2 * k - 1 + way


def kernel(
    n, nf, fetch, hubs,
    feats, edges, fetch_in_hbm, targets_in, hub_tiles_in, w_self_in, w_neigh_in, degree_in, bias_in,
    out_hbm, fetch_tiles, targets, hub_tiles, degree, bias, out, xbuf, wts, w_self, w_neigh, fetch_out, fetch_in, fetch_s, prev, last, prev2, last2, own_proj, inv, acc, acc2, hub_out, hub_in, sib_out, sib_in,
    local_sem, xs, xr, fs, fr, zs, zr, ss, sr, hs, hr, bs, br, out_sem, *ys,
):
    me = lax.axis_index("nodes")
    mf = lax.axis_index("feat")
    u = lax.axis_index("sub")
    tiles, tile, cols = feats.shape
    half = tiles // 2
    per = half // CHUNKS
    zero = (2 * n - 1) * fetch
    zero2 = n * hubs

    def rows(core, c):
        return pl.ds(core * half + c * per, per)

    def remote(src, dst, send, recv, **where):
        return pltpu.make_async_remote_copy(
            src_ref=src, dst_ref=dst, send_sem=send, recv_sem=recv,
            device_id=where, device_id_type=MESH,
        )

    def x_copy(d, c):
        return remote(
            feats.at[rows(u, c)], xbuf.at[d, pl.ds(c * per, per)],
            xs.at[d - 1, c], xr.at[d - 1, c], feat=lax.rem(mf + d, nf),
        )

    def f_copy(d):
        to = lax.rem(me + d, n)
        return remote(fetch_out.at[to], fetch_in.at[d], fs.at[d - 1], fr.at[d - 1], nodes=to)

    def z_copy(way, k, c):
        return remote(
            ys[place(way, k)].at[rows(u, c)], ys[place(way, k + 1)].at[rows(u, c)],
            zs.at[way, k, c], zr.at[way, k, c], nodes=me + 1 if way == 0 else me - 1,
        )

    def s_copy(p, c, core):
        return remote(
            ys[p].at[rows(core, c)], ys[p].at[rows(core, c)], ss.at[p, c], sr.at[p, c], sub=1 - u
        )

    def h_copy(d):
        return remote(
            hub_out.at[d], hub_in.at[d], hs.at[d - 1], hr.at[d - 1], nodes=lax.rem(me + d, n)
        )

    def b_copy(t):
        return remote(sib_out.at[t], sib_in.at[t], bs.at[t], br.at[t], sub=1 - u)

    def exists(way, k):
        return me >= k if way == 0 else me + k < n

    barrier = pltpu.get_barrier_semaphore()
    for d in range(1, nf):
        pl.semaphore_signal(barrier, inc=1, device_id={"feat": lax.rem(mf + d, nf)}, device_id_type=MESH)
    for d in range(1, n):
        pl.semaphore_signal(barrier, inc=1, device_id={"nodes": lax.rem(me + d, n)}, device_id_type=MESH)
    pl.semaphore_signal(barrier, inc=1, device_id={"sub": 1 - u}, device_id_type=MESH)
    own_copy = pltpu.make_async_copy(feats.at[pl.ds(u * half, half)], xbuf.at[0], local_sem.at[0])
    own_copy.start()
    w_copies = []
    for i, (whole, part) in enumerate(((w_neigh_in, w_neigh), (w_self_in, w_self))):
        if whole.shape[1] != cols:
            whole = whole.at[:, pl.ds(pl.multiple_of(mf * cols, cols), cols)]
        w_copies.append(pltpu.make_async_copy(whole, part, local_sem.at[3 + i]))
        w_copies[-1].start()
    wts_copy = pltpu.make_async_copy(edges, wts, local_sem.at[1])
    wts_copy.start()

    small = []
    for i, (src, dst) in enumerate((
        (fetch_in_hbm, fetch_tiles), (targets_in, targets), (hub_tiles_in, hub_tiles),
        (degree_in, degree), (bias_in, bias),
    )):
        small.append(pltpu.make_async_copy(src, dst, local_sem.at[5 + i]))
        small[-1].start()

    pl.semaphore_wait(barrier, nf + n - 1)

    for c in range(CHUNKS):
        for d in range(1, nf):
            x_copy(d, c).start()
    small[0].wait()
    fetch_out[...] = jnp.zeros_like(fetch_out)
    for t in range(n):
        fetch_out[t, 0:1, 0:fetch] = fetch_tiles[t:t + 1, :]
    for d in range(1, n):
        f_copy(d).start()
    fetch_in[0] = fetch_out[me]
    acc[zero] = jnp.zeros((tile, cols), jnp.float32)
    acc2[zero2] = jnp.zeros((tile, cols), jnp.float32)

    spots = [(0, 0)] + [(way, k) for k in range(1, n) for way in range(2)]

    def link(way, k):
        p = place(way, k)
        shard = me - k if way == 0 else me + k

        def edge(j, carry):
            target = targets[shard, j]
            slot = p * fetch + j
            prev[slot] = last[target]
            for g in range(tiles + n * hubs):
                last[g] = jnp.where(target == g, slot, last[g])
            return carry

        lax.fori_loop(0, fetch, edge, 0)

    def link_hubs():
        for g in range(tiles + n * hubs):
            last[g] = jnp.int32(zero)
        for g in range(tiles):
            last2[g] = jnp.int32(zero2)

        def helper(d, carry):
            row = lax.rem(me + n - d, n)
            for k in range(hubs):
                target = hub_tiles[row, k]
                slot = d * hubs + k
                prev2[slot] = last2[target]
                for g in range(tiles):
                    last2[g] = jnp.where(target == g, slot, last2[g])
            return carry

        lax.fori_loop(0, n, helper, 0)

    def project(w, c):
        total = None
        for d in range(nf):
            start = pl.multiple_of(lax.rem(mf + nf - d, nf) * cols, cols)
            piece = xbuf[d, c * per:(c + 1) * per].reshape(per * tile, cols)
            term = jnp.dot(piece, w[pl.ds(start, cols), :], preferred_element_type=jnp.float32)
            total = term if total is None else total + term
        return total

    own_copy.wait()
    w_copies[0].wait()
    for c in range(CHUNKS):
        for d in range(1, nf):
            x_copy(d, c).wait_recv()
        y = project(w_neigh, c)
        ys[0][rows(u, c)] = y.astype(jnp.bfloat16).reshape(per, tile, cols)
        for way in range(2):
            pl.when(exists(1 - way, 1))(lambda: z_copy(way, 0, c).start())
        s_copy(0, c, u).start()
        if c == 0:
            small[1].wait()
            small[2].wait()
            link_hubs()
        elif c <= len(spots):
            way, k = spots[c - 1]
            pl.when(exists(way, k))(functools.partial(link, way, k))
    for way, k in spots[CHUNKS - 1:]:
        pl.when(exists(way, k))(functools.partial(link, way, k))

    def prepare():
        for d in range(1, n):
            f_copy(d).wait_recv()
        to_smem = pltpu.make_async_copy(fetch_in, fetch_s, local_sem.at[2])
        to_smem.start()
        diagonal = lax.broadcasted_iota(jnp.int32, (tile, tile), 0) == lax.broadcasted_iota(
            jnp.int32, (tile, tile), 1
        )
        w_copies[1].wait()
        small[3].wait()
        small[4].wait()
        for c in range(CHUNKS):
            own_proj[c * per:(c + 1) * per] = (project(w_self, c) + bias[...]).reshape(per, tile, cols)
        for t in range(half):
            row = 1.0 / degree[pl.ds(u * half + t, 1), :].astype(jnp.float32)
            inv[t] = jnp.sum(
                jnp.where(diagonal, jnp.broadcast_to(row, (tile, tile)), 0.0), axis=1, keepdims=True
            )
        wts_copy.wait()
        to_smem.wait()

    def contribute(way, k):
        p = place(way, k)
        shard = me - k if way == 0 else me + k
        d = k if way == 0 else (n - k) % n
        for c in range(CHUNKS):
            s_copy(p, c, 1 - u).wait_recv()
        for j in range(fetch):
            term = jnp.dot(
                wts[shard, j], ys[p][fetch_s[d, 0, j]], preferred_element_type=jnp.float32
            )
            acc[p * fetch + j] = acc[prev[p * fetch + j]] + term

    def arrive(way, k, c):
        z_copy(way, k - 1, c).wait_recv()
        if k < n - 1:
            pl.when(exists(1 - way, 1))(lambda: z_copy(way, k, c).start())
        s_copy(place(way, k), c, u).start()

    for k in range(1, n):
        for c in range(CHUNKS):
            for way in range(2):
                pl.when(exists(way, k))(functools.partial(arrive, way, k, c))
            if c == 0 and k > 1:
                for way in range(2):
                    pl.when(exists(way, k - 1))(functools.partial(contribute, way, k - 1))
        if k == 1:
            prepare()
            contribute(0, 0)
    for way in range(2):
        pl.when(exists(way, n - 1))(functools.partial(contribute, way, n - 1))

    def put_hubs(d):
        to = lax.rem(me + d, n)
        for k in range(hubs):
            part = acc[last[tiles + to * hubs + k]].astype(jnp.bfloat16)
            if d:
                hub_out[d, k] = part
            else:
                hub_in[0, k] = part

    def sent(way, k, c):
        z_copy(way, k, c).wait_send()

    for d in range(n):
        put_hubs(d)
    inside = (me > 0) & (me < n - 1)
    for d in range(1, n):
        to = lax.rem(me + d, n)
        pl.when(inside & (to > 0) & (to < n - 1))(lambda: h_copy(d).start())
    for c in range(CHUNKS):
        for way in range(2):
            for k in range(n - 1):
                pl.when(exists(way, k) & exists(1 - way, 1))(functools.partial(sent, way, k, c))
    for d in range(1, n):
        to = lax.rem(me + d, n)
        pl.when(inside & ((to == 0) | (to == n - 1)))(lambda: h_copy(d).start())
        pl.when(me == n - 1)(lambda: h_copy(d).start())
        pl.when(me == 0)(lambda: h_copy(n - d).start())

    for d in range(n):
        if d:
            h_copy(d).wait_recv()
        for k in range(hubs):
            acc2[d * hubs + k] = acc2[prev2[d * hubs + k]] + hub_in[d, k].astype(
                jnp.float32
            )

    def o_copy(t):
        return pltpu.make_async_copy(out.at[t], out_hbm.at[t], out_sem.at[t])

    def total(t):
        return acc[last[t]] + acc2[last2[t]]

    for t in range(half):
        sib_out[t] = total((1 - u) * half + t).astype(jnp.bfloat16)
        b_copy(t).start()
    for t in range(half):
        mine = total(u * half + t)
        b_copy(t).wait_recv()
        pre = own_proj[t] + (mine + sib_in[t].astype(jnp.float32)) * inv[t]
        out[t] = pre.astype(jnp.bfloat16)
        o_copy(t).start()

    for c in range(CHUNKS):
        for d in range(1, nf):
            x_copy(d, c).wait_send()
    for d in range(1, n):
        f_copy(d).wait_send()
        h_copy(d).wait_send()
    for t in range(half):
        b_copy(t).wait_send()
        o_copy(t).wait()

    for c in range(CHUNKS):
        s_copy(0, c, u).wait_send()
        for way in range(2):
            for k in range(1, n):
                pl.when(exists(way, k))(lambda: s_copy(place(way, k), c, u).wait_send())


def body(
    features, fetch_tiles, edge_weights, target_slots, hub_tiles, degree, w_self, w_neigh, bias
):
    n = lax.axis_size("nodes")
    nf = lax.axis_size("feat")
    cols = features.shape[1]
    tile = edge_weights.shape[-1]
    tiles = features.shape[0] // tile
    half = tiles // 2
    fetch = fetch_tiles.shape[2]
    hubs = hub_tiles.shape[2]
    if cols % 128:
        first_col = lax.axis_index("feat") * cols
        w_self = lax.dynamic_slice_in_dim(w_self, first_col, cols, 1)
        w_neigh = lax.dynamic_slice_in_dim(w_neigh, first_col, cols, 1)
    depth = w_self.shape[0]

    bf16, f32 = jnp.bfloat16, jnp.float32
    hbm = pl.BlockSpec(memory_space=pl.ANY)
    dma = pltpu.SemaphoreType.DMA
    result = pl.pallas_call(
        functools.partial(kernel, n, nf, fetch, hubs),
        out_shape=jax.ShapeDtypeStruct((half, tile, cols), bf16),
        in_specs=[hbm] * 9,
        out_specs=hbm,
        scratch_shapes=[
            pltpu.VMEM((n, fetch), jnp.int32),
            pltpu.SMEM((n, fetch), jnp.int32),
            pltpu.SMEM((n, hubs), jnp.int32),
            pltpu.VMEM((tiles, tile), jnp.int32),
            pltpu.VMEM((1, cols), f32),
            pltpu.VMEM((half, tile, cols), bf16),
            pltpu.VMEM((nf, half, tile, cols), bf16),
            pltpu.VMEM((n, fetch, tile, tile), bf16),
            pltpu.VMEM((depth, cols), bf16),
            pltpu.VMEM((depth, cols), bf16),
            pltpu.VMEM((n, 8, 128), jnp.int32),
            pltpu.VMEM((n, 8, 128), jnp.int32),
            pltpu.SMEM((n, 8, 128), jnp.int32),
            pltpu.SMEM(((2 * n - 1) * fetch,), jnp.int32),
            pltpu.SMEM((tiles + n * hubs,), jnp.int32),
            pltpu.SMEM((n * hubs,), jnp.int32),
            pltpu.SMEM((tiles,), jnp.int32),
            pltpu.VMEM((half, tile, cols), f32),
            pltpu.VMEM((half, tile, 1), f32),
            pltpu.VMEM(((2 * n - 1) * fetch + 1, tile, cols), f32),
            pltpu.VMEM((n * hubs + 1, tile, cols), f32),
            pltpu.VMEM((n, hubs, tile, cols), bf16),
            pltpu.VMEM((n, hubs, tile, cols), bf16),
            pltpu.VMEM((half, tile, cols), bf16),
            pltpu.VMEM((half, tile, cols), bf16),
            dma((10,)),
            dma((nf - 1, CHUNKS)),
            dma((nf - 1, CHUNKS)),
            dma((n - 1,)),
            dma((n - 1,)),
            dma((2, n - 1, CHUNKS)),
            dma((2, n - 1, CHUNKS)),
            dma((2 * n - 1, CHUNKS)),
            dma((2 * n - 1, CHUNKS)),
            dma((n - 1,)),
            dma((n - 1,)),
            dma((half,)),
            dma((half,)),
            dma((half,)),
        ]
        + [pltpu.VMEM((tiles, tile, cols), bf16) for _ in range(2 * n - 1)],
        compiler_params=pltpu.CompilerParams(
            collective_id=0, has_side_effects=True, vmem_limit_bytes=56 * 1024 * 1024
        ),
        name="sage_layer",
    )(
        features.reshape(tiles, tile, cols), edge_weights[0], fetch_tiles[0], target_slots[0],
        hub_tiles[0], w_self, w_neigh, degree.reshape(tiles, tile), bias.reshape(1, cols),
    )
    return jnp.maximum(result.reshape(half * tile, cols), 0)


def solution(mesh):
    return jax.shard_map(
        body,
        mesh=mesh,
        in_specs=(
            P(("parts", "nodes"), "feat"),
            P(("parts", "nodes"), None, "sub"),
            P(("parts", "nodes"), None, "sub", None, None),
            P(("parts", "nodes"), None, "sub"),
            P(("parts", "nodes"), None, "sub"),
            P(("parts", "nodes")),
            P(),
            P(),
            P("feat"),
        ),
        out_specs=P(("parts", "nodes", "sub"), "feat"),
        check_vma=False,
    )
```
